32 devices in a mesh: grp: 2 (over x), ep: 16 (over z, y, core).
Axes of the slice: x: 2, y: 2, z: 4, core: 2. Of those that a mesh axis runs over, the one named last changes fastest.
Arguments:
- page_key_value_codes: bfloat16 [1024, 32, 1024], P(('grp', 'ep')), parts along dimension 0, may hold values from -6 to 6
- page_key_scales: bfloat16 [1024, 2], P(('grp', 'ep')), parts along dimension 0, may hold values from 0.5 to 2
- page_value_scales: bfloat16 [1024, 2], P(('grp', 'ep')), parts along dimension 0, may hold values from 4 to 32
- block_table: int32 [32, 32], P('grp', 'ep'), parts along dimension 0, may hold values from 0 to 31, as said below
- prompt_lengths: int32 [32], P('grp'), parts along dimension 0, may hold values from 512 to 1024, as said below
- decode_owner: int32 [32], P('grp'), parts along dimension 0, may hold values from 0 to 15, each once
- prefill_states: bfloat16 [32, 32, 128, 128], P('grp', 'ep'), parts along dimension 0, may hold values from -48 to 48
- att_query: bfloat16 [512, 4, 2048], P(('grp', 'ep')), parts along dimension 0, may hold values from -144 to 144
- att_gate: bfloat16 [512, 4, 2048], P(('grp', 'ep')), parts along dimension 0, may hold values from -6 to 6
- draft_keys_values: bfloat16 [512, 4, 1024], P(('grp', 'ep')), parts along dimension 0, may hold values from -24 to 24
- out_weight: bfloat16 [2048, 2048], replicated, may hold values from -0.125 to 0.125
- residual: bfloat16 [512, 4, 2048], P(('grp', 'ep')), parts along dimension 0, may hold values from -6 to 6
- norm_gain: bfloat16 [2048], replicated, may hold values from 0.099609375 to 1.8984375
- router_weight: bfloat16 [2048, 16], replicated, may hold values from -0.125 to 0.125
- expert_routes: int32 [512, 4, 8], P(('grp', 'ep')), parts along dimension 0, may hold values from 0 to 15, all different within a row; in each aligned block of 64 rows (0 to 63, 64 to 127, ..., all dimensions but the last counted through in order) at most 32 rows name the same one
- gate_weight: bfloat16 [16, 2048, 512], P('ep'), may hold values from -0.125 to 0.125
- up_weight: bfloat16 [16, 2048, 512], P('ep'), may hold values from -0.125 to 0.125
- down_weight: bfloat16 [16, 512, 2048], P('ep'), may hold values from -0.25 to 0.25
- gdn_qk: bfloat16 [512, 4, 4096], P(('grp', 'ep')), parts along dimension 0, may hold values from -8.4 to 8.4
- gdn_v: bfloat16 [512, 4, 4096], P(('grp', 'ep')), parts along dimension 0, may hold values from -12 to 12
- gdn_decay: float32 [512, 4, 32], P(('grp', 'ep')), parts along dimension 0, may hold values from 0.5 to 1
- gdn_beta: float32 [512, 4, 32], P(('grp', 'ep')), parts along dimension 0, may hold values from 0.1 to 1
Outputs:
- attn_mix: bfloat16 [512, 4, 2048], P(('grp', 'ep')), parts along dimension 0
- moe_out: bfloat16 [512, 4, 2048], P(('grp', 'ep')), parts along dimension 0
- gdn_out: bfloat16 [512, 4, 4096], P(('grp', 'ep')), parts along dimension 0
The draws below stay inside these ranges and needn't reach their ends.
There are 2 independent parts, one for each index of `grp`. The reference program is written for one: setup_inputs(seed, part) draws one part's arguments, and reference() takes and returns one part's arrays. A program takes and returns all parts, laid end to end along the dimension named above; an argument that names none is the same for every part. Nothing has to cross between parts.
Inputs may be any that keep to these rules, and one draw needn't show every extreme that they name: `block_table`: the 2 columns of one ep device name each of that device's 16 * 2 pages once. `prompt_lengths`: some prompt is 1024 long. `decode_owner`: each device decodes exactly one prompt. `expert_routes`: the 8 experts of one row and draft differ; among the 64 row-draft pairs of one decode device no expert is named more than 32 times, and one is named exactly 32 times in some devices' rows.
All inputs are finite; a program needn't handle non-finite values.
Results may differ from the reference program's by a relative error of at most 0.011.
Values may be sent and summed in bfloat16 or wider, within the bound.
A program may use at most 128 MiB of HBM per device.

```python
import math
import jax
import jax.numpy as jnp
import numpy as np
from jax import lax

D = 2048
QUERY_HEADS = 8
KEY_VALUE_HEADS = 2
HEAD_SIZE = 256
DH = 32
KH = 16
DK = 128
DV = 128
FFE = 512
TOPK = 8
CAP = 32
PAGE_POSITIONS = 32
DRAFT_POSITIONS = 4
BEAMS = 16
EXPERTS = 16
PROMPTS = 16
PROMPT_POSITIONS = 1024
BLKS_DEV = 2
NBLK = 32
TOTAL_PAGES = 512
DECODE_ROWS = 256
N_EP = 16


def draw_block_table(key, part):
    key = jax.random.fold_in(key, 7)
    device_count = NBLK // BLKS_DEV
    key_list = jax.random.split(key, device_count)
    orders = jax.vmap(lambda one_key: jax.random.permutation(one_key, PROMPTS * BLKS_DEV))(key_list)
    orders = orders.reshape(device_count, PROMPTS, BLKS_DEV).transpose(1, 0, 2).reshape(PROMPTS, NBLK)
    return orders.astype(jnp.int32)


def draw_prompt_lengths(key, part):
    key = jax.random.fold_in(key, 11)
    length_key, top_key = jax.random.split(key)
    lengths = jax.random.randint(length_key, (PROMPTS,), PROMPT_POSITIONS // 2, PROMPT_POSITIONS + 1)
    longest = jax.random.randint(top_key, (), 0, PROMPTS)
    lengths = jnp.where(jnp.arange(PROMPTS) == longest, PROMPT_POSITIONS, lengths)
    return lengths.astype(jnp.int32)


def draw_att_query(key, part):
    key = jax.random.fold_in(key, 5)
    base_key = jax.random.fold_in(key, 0)
    samples = jax.random.truncated_normal(base_key, -6.0, 6.0, (DECODE_ROWS, DRAFT_POSITIONS, QUERY_HEADS * HEAD_SIZE), jnp.float32)
    return samples.astype(jnp.bfloat16)


def draw_gdn_qk(key, part):
    key = jax.random.fold_in(key, 9)
    key_part, noise_part = jax.random.split(key)
    full_shape = (DECODE_ROWS, DRAFT_POSITIONS, KH * DK)
    rows_of_keys = jax.random.truncated_normal(key_part, -6.0, 6.0, full_shape, jnp.float32)
    noise_rows = jax.random.truncated_normal(noise_part, -6.0, 6.0, full_shape, jnp.float32)
    query_vectors = 0.6 * rows_of_keys + 0.8 * noise_rows
    return jnp.concatenate([query_vectors, rows_of_keys], axis=-1).astype(jnp.bfloat16)


def steps_of(stream_key, shape, cuts, least, top_value):
    def one(dim, parts):
        steps = jax.random.uniform(jax.random.fold_in(jax.random.fold_in(stream_key, 6), dim), (parts,), jnp.float32, least / len(cuts), top_value / len(cuts))
        return jnp.repeat(jnp.exp(steps), shape[dim] // parts).reshape((-1,) + (1,) * (len(shape) - dim - 1))

    factor_of = one(*cuts[0])
    for cut in cuts[1:]:
        factor_of = factor_of * one(*cut)
    return factor_of


def deal_out(stream_key, own, number, rows, number_of, top, bound, lean):
    ranking = jax.random.permutation(stream_key, number_of)
    crowded, ordinary = shares(number_of, rows * top, bound, lean, True), shares(number_of, rows * top, bound, lean, False)
    places = jnp.arange(number_of)

    def named(sizes, offset_by):
        used = int((sizes > 0).sum())
        fixed = max(1, used // 4)
        moved = fixed + (places - fixed + offset_by * (used - fixed)) % max(1, number_of - fixed)
        return jnp.zeros((number_of,), jnp.int32).at[ranking[jnp.where(places < fixed, places, moved)]].set(jnp.asarray(sizes, jnp.int32))

    sizes = jnp.where(number % 4 == 0, named(crowded, number // 4), named(ordinary, number - number // 4 - 1))
    mixed = jax.random.permutation(jax.random.fold_in(own, 3), number_of)
    donor, taker = mixed[0:number_of // 2 * 2:2], mixed[1:number_of // 2 * 2:2]
    slack = jnp.minimum(sizes[donor] - 1, bound - sizes[taker]) // 2
    slack = jnp.where((donor == ranking[0]) | (taker == ranking[0]) | (sizes[taker] == 0), 0, jnp.maximum(slack, 0))
    moved = jax.random.randint(jax.random.fold_in(own, 4), (number_of // 2,), 0, 1 << 20) % (slack + 1)
    sizes = sizes.at[donor].add(-moved).at[taker].add(moved)
    items = jnp.searchsorted(jnp.cumsum(sizes), jnp.arange(rows * top), side="right").astype(jnp.int32)
    listing = items.reshape(top, rows).T
    listing = listing[jax.random.permutation(jax.random.fold_in(own, 1), rows)]
    offset_by = jax.random.randint(jax.random.fold_in(own, 2), (rows, 1), 0, top)
    return jnp.take_along_axis(listing, (jnp.arange(top)[None, :] + offset_by) % top, axis=1)


def shares(number_of, total, limit, lean, full):
    loads = [(1 << 20) // math.isqrt(rank ** lean) + 1 for rank in range(1, number_of + 1)]
    largest = limit if full else min(limit, max(-(-total // number_of), total * loads[0] // sum(loads)))
    least = 1 if total - largest >= number_of - 1 else 0
    holding, surplus = [largest] + [least] * (number_of - 1), total - largest - least * (number_of - 1)
    while surplus > 0:
        candidates = [i for i in range(1, number_of) if holding[i] < largest] or [i for i in range(1, number_of) if holding[i] < limit]
        pool, remaining = sum([loads[i] for i in candidates]), surplus
        for i in candidates:
            extra = min(limit - holding[i], max(1, remaining * loads[i] // pool), surplus)
            holding[i] = holding[i] + extra
            surplus = surplus - extra
    return np.array(holding)


def gaussian(key, dims, width, reach, cuts=(), kind=jnp.bfloat16):
    drawn = width * jax.random.normal(key, dims, jnp.float32)
    if cuts:
        drawn = drawn * steps_of(key, dims, cuts, -0.22, 0.18)
    return jnp.clip(drawn, -reach, reach).astype(kind)


def setup_inputs(seed: int = 0, part: int = 0) -> dict:
    key_of = jax.random.split(jax.random.key(seed), 23)
    part_keys = jax.random.split(jax.random.fold_in(key_of[22], part), 23)
    page_key_value_codes = gaussian(part_keys[0], (TOTAL_PAGES, PAGE_POSITIONS, 2 * KEY_VALUE_HEADS * HEAD_SIZE), 1.0, 6.0, ((0, 16),))
    page_key_scales = jnp.clip(jnp.exp(math.log(2.0) - 1.3862944 * jax.random.uniform(part_keys[1], (TOTAL_PAGES, KEY_VALUE_HEADS), jnp.float32) ** steps_of(part_keys[1], (TOTAL_PAGES, KEY_VALUE_HEADS), ((0, 16),), -0.2, 0.2)), 0.5, 2.0).astype(jnp.bfloat16)
    page_value_scales = jnp.clip(jnp.exp(math.log(32.0) - 2.0794415 * jax.random.uniform(part_keys[2], (TOTAL_PAGES, KEY_VALUE_HEADS), jnp.float32) ** steps_of(part_keys[2], (TOTAL_PAGES, KEY_VALUE_HEADS), ((0, 16),), -0.2, 0.2)), 4.0, 32.0).astype(jnp.bfloat16)
    block_table = draw_block_table(jax.random.fold_in(jax.random.fold_in(key_of[22], part), 71), part)
    prompt_lengths = draw_prompt_lengths(jax.random.fold_in(jax.random.fold_in(key_of[22], part), 71), part)
    decode_owner = jax.random.permutation(part_keys[5], PROMPTS).astype(jnp.int32)
    prefill_states = gaussian(part_keys[6], (PROMPTS, DH, DK, DV), 8.0, 48.0, ((1, 16),))
    att_query = draw_att_query(jax.random.fold_in(jax.random.fold_in(key_of[22], part), 71), part)
    att_gate = gaussian(part_keys[8], (DECODE_ROWS, DRAFT_POSITIONS, QUERY_HEADS * HEAD_SIZE), 1.0, 6.0, ((0, 16),))
    draft_keys_values = gaussian(part_keys[9], (DECODE_ROWS, DRAFT_POSITIONS, 2 * KEY_VALUE_HEADS * HEAD_SIZE), 4.0, 24.0, ((0, 16),))
    out_weight = gaussian(key_of[10], (QUERY_HEADS * HEAD_SIZE, D), (QUERY_HEADS * HEAD_SIZE) ** -0.5, 0.125)
    residual = gaussian(part_keys[11], (DECODE_ROWS, DRAFT_POSITIONS, D), 1.0, 6.0, ((0, 16),))
    norm_gain = jnp.clip(1.0 + 0.18 * jax.random.normal(key_of[12], (D,), jnp.float32), 0.099609375, 1.8984375).astype(jnp.bfloat16)
    router_weight = gaussian(key_of[13], (D, EXPERTS), D ** -0.5, 0.125)
    expert_routes_keys = jax.random.split(jax.random.fold_in(part_keys[14], 1), DECODE_ROWS * DRAFT_POSITIONS // (BEAMS * DRAFT_POSITIONS))
    expert_routes_turns = jax.random.permutation(jax.random.fold_in(part_keys[14], 3), DECODE_ROWS * DRAFT_POSITIONS // (BEAMS * DRAFT_POSITIONS))
    expert_routes = jax.vmap(lambda own, number: deal_out(jax.random.fold_in(part_keys[14], 2), own, number, BEAMS * DRAFT_POSITIONS, EXPERTS, TOPK, CAP, 2))(expert_routes_keys, expert_routes_turns).reshape((DECODE_ROWS, DRAFT_POSITIONS, TOPK))
    gate_weight = gaussian(key_of[15], (EXPERTS, D, FFE), D ** -0.5, 0.125, ((0, 16),))
    up_weight = gaussian(key_of[16], (EXPERTS, D, FFE), D ** -0.5, 0.125, ((0, 16),))
    down_weight = gaussian(key_of[17], (EXPERTS, FFE, D), FFE ** -0.5, 0.25, ((0, 16),))
    gdn_qk = draw_gdn_qk(jax.random.fold_in(jax.random.fold_in(key_of[22], part), 71), part)
    gdn_v = gaussian(part_keys[19], (DECODE_ROWS, DRAFT_POSITIONS, DH * DV), 2.0, 12.0, ((0, 16),))
    gdn_decay = jnp.clip(0.5 + 0.5 * jax.random.uniform(part_keys[20], (DECODE_ROWS, DRAFT_POSITIONS, DH), jnp.float32) ** steps_of(part_keys[20], (DECODE_ROWS, DRAFT_POSITIONS, DH), ((0, 16),), -0.2, 0.2), 0.5, 1.0)
    gdn_beta = jnp.clip(0.1 + 0.9 * jax.random.uniform(part_keys[21], (DECODE_ROWS, DRAFT_POSITIONS, DH), jnp.float32) ** steps_of(part_keys[21], (DECODE_ROWS, DRAFT_POSITIONS, DH), ((0, 16),), -0.2, 0.2), 0.1, 1.0)
    return {"page_key_value_codes": page_key_value_codes, "page_key_scales": page_key_scales, "page_value_scales": page_value_scales, "block_table": block_table, "prompt_lengths": prompt_lengths, "decode_owner": decode_owner, "prefill_states": prefill_states, "att_query": att_query, "att_gate": att_gate, "draft_keys_values": draft_keys_values, "out_weight": out_weight, "residual": residual, "norm_gain": norm_gain, "router_weight": router_weight, "expert_routes": expert_routes, "gate_weight": gate_weight, "up_weight": up_weight, "down_weight": down_weight, "gdn_qk": gdn_qk, "gdn_v": gdn_v, "gdn_decay": gdn_decay, "gdn_beta": gdn_beta}


norm_eps = 1e-06
masked_score = -1e+30

def owner_inverse(decode_owner):
    labels = jnp.arange(decode_owner.shape[0], dtype=jnp.int32)
    matches = (decode_owner[:, None] == labels[None, :]).astype(jnp.int32)
    return lax.optimization_barrier(jnp.sum(labels[:, None] * matches, axis=0)).astype(jnp.int32)

def attend_prompt(rows_of_queries, gate_rows, fresh_keys_values, codes_by_row, scale_of_key, scale_of_value, length):
    beam_total = rows_of_queries.shape[0]
    draft_tokens = rows_of_queries.shape[1]
    query_groups = QUERY_HEADS // KEY_VALUE_HEADS
    span_length = codes_by_row.shape[0]
    query_vectors = rows_of_queries.astype(jnp.float32).reshape(beam_total, draft_tokens, KEY_VALUE_HEADS, query_groups, HEAD_SIZE)
    rows_of_keys = codes_by_row[:, :KEY_VALUE_HEADS * HEAD_SIZE].astype(jnp.float32).reshape(span_length, KEY_VALUE_HEADS, HEAD_SIZE)
    rows_of_values = codes_by_row[:, KEY_VALUE_HEADS * HEAD_SIZE:].astype(jnp.float32).reshape(span_length, KEY_VALUE_HEADS, HEAD_SIZE)
    key_pos = jnp.repeat(scale_of_key.astype(jnp.float32), PAGE_POSITIONS, axis=0).T
    value_pos = jnp.repeat(scale_of_value.astype(jnp.float32), PAGE_POSITIONS, axis=0).T
    fresh_keys = fresh_keys_values[:, :, :KEY_VALUE_HEADS * HEAD_SIZE].astype(jnp.float32).reshape(beam_total, draft_tokens, KEY_VALUE_HEADS, HEAD_SIZE)
    fresh_values = fresh_keys_values[:, :, KEY_VALUE_HEADS * HEAD_SIZE:].astype(jnp.float32).reshape(beam_total, draft_tokens, KEY_VALUE_HEADS, HEAD_SIZE)
    factor = HEAD_SIZE ** (-0.5)
    cached = jnp.einsum('btgqd,lgd->btgql', query_vectors, rows_of_keys) * key_pos[None, None, :, None, :] * factor
    live_mask = jnp.arange(span_length, dtype=jnp.int32) < length
    cached = jnp.where(live_mask[None, None, None, None, :], cached, masked_score)
    own_scores = jnp.einsum('btgqd,bsgd->btgqs', query_vectors, fresh_keys) * factor
    draft_order = jnp.arange(draft_tokens, dtype=jnp.int32)
    causal = draft_order[:, None] >= draft_order[None, :]
    own_scores = jnp.where(causal[None, :, None, None, :], own_scores, masked_score)
    top_score = jnp.maximum(lax.optimization_barrier(jnp.max(cached, axis=-1)), lax.optimization_barrier(jnp.max(own_scores, axis=-1)))[..., None]
    cached_exp = jnp.exp(cached - top_score)
    own_exp = jnp.exp(own_scores - top_score)
    total = lax.optimization_barrier(jnp.sum(cached_exp, axis=-1, keepdims=True)) + lax.optimization_barrier(jnp.sum(own_exp, axis=-1, keepdims=True))
    cached_w = (cached_exp / total * value_pos[None, None, :, None, :]).astype(jnp.bfloat16)
    own_w = (own_exp / total).astype(jnp.bfloat16)
    mixed = jnp.einsum('btgql,lgd->btgqd', cached_w.astype(jnp.float32), rows_of_values)
    mixed = mixed + jnp.einsum('btgqs,bsgd->btgqd', own_w.astype(jnp.float32), fresh_values)
    mixed = mixed.reshape(beam_total, draft_tokens, QUERY_HEADS * HEAD_SIZE)
    return (mixed * jax.nn.sigmoid(gate_rows.astype(jnp.float32))).astype(jnp.bfloat16)

def expert_rows(received, gate_w, up_w, down_w):
    model_width = received.shape[-1]
    flat_rows = received.reshape(-1, model_width)
    gate_val = jnp.dot(flat_rows, gate_w, preferred_element_type=jnp.float32)
    up_val = jnp.dot(flat_rows, up_w, preferred_element_type=jnp.float32)
    inner_act = (jax.nn.silu(gate_val) * up_val).astype(jnp.bfloat16)
    produced = jnp.dot(inner_act, down_w, preferred_element_type=jnp.float32).astype(jnp.bfloat16)
    return produced.reshape(received.shape)

def normalize(vectors):
    return vectors * lax.rsqrt(lax.optimization_barrier(jnp.sum(vectors * vectors, axis=-1, keepdims=True)) + norm_eps)

def reference(page_key_value_codes, page_key_scales, page_value_scales, block_table, prompt_lengths, decode_owner, prefill_states, att_query, att_gate, draft_keys_values, out_weight, residual, norm_gain, router_weight, expert_routes, gate_weight, up_weight, down_weight, gdn_qk, gdn_v, gdn_decay, gdn_beta):
    inverse = owner_inverse(decode_owner)
    pages_dev = PROMPTS * BLKS_DEV
    home_page = jnp.arange(NBLK, dtype=jnp.int32) // BLKS_DEV * pages_dev

    def attend_device(device_id):
        prompt_id = inverse[device_id]
        rows_of_pages = home_page + block_table[prompt_id]
        codes_by_row = page_key_value_codes[rows_of_pages].reshape(PROMPT_POSITIONS, 2 * KEY_VALUE_HEADS * HEAD_SIZE)
        row_start = device_id * BEAMS
        rows_of_queries = lax.dynamic_slice_in_dim(att_query, row_start, BEAMS, 0)
        gate_rows = lax.dynamic_slice_in_dim(att_gate, row_start, BEAMS, 0)
        fresh_keys_values = lax.dynamic_slice_in_dim(draft_keys_values, row_start, BEAMS, 0)
        return attend_prompt(rows_of_queries, gate_rows, fresh_keys_values, codes_by_row, page_key_scales[rows_of_pages], page_value_scales[rows_of_pages], prompt_lengths[prompt_id])
    gated_out = lax.map(attend_device, jnp.arange(N_EP, dtype=jnp.int32))
    row_count = DECODE_ROWS * DRAFT_POSITIONS
    attn_mix = jnp.dot(gated_out.reshape(row_count, QUERY_HEADS * HEAD_SIZE), out_weight, preferred_element_type=jnp.float32).astype(jnp.bfloat16)
    hidden = residual.astype(jnp.float32).reshape(row_count, D) + attn_mix.astype(jnp.float32)
    normed = (hidden * lax.rsqrt(lax.optimization_barrier(jnp.mean(hidden * hidden, axis=-1, keepdims=True)) + norm_eps) * norm_gain.astype(jnp.float32)).astype(jnp.bfloat16)
    logits = jnp.dot(normed, router_weight, preferred_element_type=jnp.float32)
    routes = expert_routes.reshape(row_count, TOPK)
    mixing = jax.nn.softmax(jnp.take_along_axis(logits, routes, axis=1), axis=-1)
    per_device = expert_routes.reshape(N_EP, BEAMS * DRAFT_POSITIONS * TOPK)
    labels = jnp.arange(EXPERTS, dtype=jnp.int32)
    matches = (per_device[:, :, None] == labels[None, None, :]).astype(jnp.int32)
    earlier = jnp.cumsum(matches, axis=1) - matches
    slot_ids = lax.optimization_barrier(jnp.sum(earlier * matches, axis=2))
    sources = jnp.arange(N_EP, dtype=jnp.int32)[:, None]
    target = (per_device * (N_EP * CAP) + sources * CAP + slot_ids).reshape(-1).astype(jnp.int32)
    owners = jnp.arange(row_count * TOPK, dtype=jnp.int32) // TOPK
    slot_table = jnp.full((EXPERTS * N_EP * CAP,), row_count, jnp.int32).at[target].set(owners)
    padded = jnp.concatenate([normed, jnp.zeros((1, D), jnp.bfloat16)], axis=0)
    buffers = padded[slot_table].reshape(EXPERTS, N_EP * CAP, D)

    def expert_apply(pieces):
        return expert_rows(pieces[0], pieces[1], pieces[2], pieces[3])
    produced = lax.map(expert_apply, (buffers, gate_weight, up_weight, down_weight))
    returned = produced.reshape(EXPERTS * N_EP * CAP, D)[target].reshape(row_count, TOPK, D)
    moe_out = lax.optimization_barrier(jnp.sum(mixing[:, :, None] * returned.astype(jnp.float32), axis=1)).astype(jnp.bfloat16)

    def delta_device(device_id):
        prompt_id = inverse[device_id]
        row_start = device_id * BEAMS
        qk_rows = lax.dynamic_slice_in_dim(gdn_qk, row_start, BEAMS, 0).astype(jnp.float32)
        rows_of_values = lax.dynamic_slice_in_dim(gdn_v, row_start, BEAMS, 0).astype(jnp.float32)
        decay_rows = lax.dynamic_slice_in_dim(gdn_decay, row_start, BEAMS, 0)
        rate_rows = lax.dynamic_slice_in_dim(gdn_beta, row_start, BEAMS, 0)
        current_state = jnp.broadcast_to(prefill_states[prompt_id].astype(jnp.float32)[None], (BEAMS, DH, DK, DV))
        outputs = []
        for draft_idx in range(DRAFT_POSITIONS):
            query_vec = normalize(qk_rows[:, draft_idx, :KH * DK].reshape(BEAMS, KH, DK)) * DK ** (-0.5)
            key_vec = normalize(qk_rows[:, draft_idx, KH * DK:].reshape(BEAMS, KH, DK))
            query_vec = jnp.repeat(query_vec, DH // KH, axis=1)
            key_vec = jnp.repeat(key_vec, DH // KH, axis=1)
            current_state = decay_rows[:, draft_idx][:, :, None, None] * current_state
            update = rows_of_values[:, draft_idx].reshape(BEAMS, DH, DV) - jnp.einsum('bhkv,bhk->bhv', current_state, key_vec, precision=lax.Precision.HIGHEST)
            current_state = current_state + rate_rows[:, draft_idx][:, :, None, None] * key_vec[:, :, :, None] * update[:, :, None, :]
            outputs.append(jnp.einsum('bhkv,bhk->bhv', current_state, query_vec, precision=lax.Precision.HIGHEST).reshape(BEAMS, DH * DV))
        return jnp.stack(outputs, axis=1).astype(jnp.bfloat16)
    gdn_out = lax.map(delta_device, jnp.arange(N_EP, dtype=jnp.int32)).reshape(DECODE_ROWS, DRAFT_POSITIONS, DH * DV)
    return (attn_mix.reshape(DECODE_ROWS, DRAFT_POSITIONS, D), moe_out.reshape(DECODE_ROWS, DRAFT_POSITIONS, D), gdn_out)
```

```python
import functools

import jax
import jax.numpy as jnp
from jax import lax
from jax.experimental import pallas as pl
from jax.experimental.pallas import tpu as pltpu
from jax.sharding import PartitionSpec as P

MESH = pl.DeviceIdType.MESH
MIX_COLUMNS = 128

QUERY_HEADS = 8
KEY_VALUE_HEADS = 2
HEAD_SIZE = 256
DK = 128
TOPK = 8
CAP = 32
PAGE_POSITIONS = 32


norm_eps = 1e-06
masked_score = -1e30


def attend_prompt(
    rows_of_queries,
    gate_rows,
    fresh_keys_values,
    codes_by_row,
    scale_of_key,
    scale_of_value,
    length,
):
    beam_total = rows_of_queries.shape[0]
    draft_tokens = rows_of_queries.shape[1]
    query_groups = QUERY_HEADS // KEY_VALUE_HEADS
    span_length = codes_by_row.shape[0]
    query_vectors = rows_of_queries.reshape(
        beam_total, draft_tokens, KEY_VALUE_HEADS, query_groups, HEAD_SIZE
    )
    rows_of_keys = codes_by_row[:, : KEY_VALUE_HEADS * HEAD_SIZE].reshape(
        span_length, KEY_VALUE_HEADS, HEAD_SIZE
    )
    rows_of_values = codes_by_row[:, KEY_VALUE_HEADS * HEAD_SIZE :].reshape(
        span_length, KEY_VALUE_HEADS, HEAD_SIZE
    )
    key_pos = jnp.repeat(scale_of_key.astype(jnp.float32), PAGE_POSITIONS, axis=0).T
    value_pos = jnp.repeat(scale_of_value.astype(jnp.float32), PAGE_POSITIONS, axis=0).T
    fresh_keys = fresh_keys_values[:, :, : KEY_VALUE_HEADS * HEAD_SIZE].reshape(
        beam_total, draft_tokens, KEY_VALUE_HEADS, HEAD_SIZE
    )
    fresh_values = fresh_keys_values[:, :, KEY_VALUE_HEADS * HEAD_SIZE :].reshape(
        beam_total, draft_tokens, KEY_VALUE_HEADS, HEAD_SIZE
    )
    factor = HEAD_SIZE ** (-0.5)
    cached = (
        jnp.einsum(
            "btgqd,lgd->btgql", query_vectors, rows_of_keys, preferred_element_type=jnp.float32
        )
        * key_pos[None, None, :, None, :]
        * factor
    )
    live_mask = jnp.arange(span_length, dtype=jnp.int32) < length
    cached = jnp.where(live_mask[None, None, None, None, :], cached, masked_score)
    own_scores = (
        jnp.einsum(
            "btgqd,bsgd->btgqs", query_vectors, fresh_keys, preferred_element_type=jnp.float32
        )
        * factor
    )
    draft_order = jnp.arange(draft_tokens, dtype=jnp.int32)
    causal = draft_order[:, None] >= draft_order[None, :]
    own_scores = jnp.where(causal[None, :, None, None, :], own_scores, masked_score)
    top_score = jnp.maximum(jnp.max(cached, axis=-1), jnp.max(own_scores, axis=-1))[..., None]
    cached_exp = jnp.exp(cached - top_score)
    own_exp = jnp.exp(own_scores - top_score)
    total = jnp.sum(cached_exp, axis=-1, keepdims=True) + jnp.sum(own_exp, axis=-1, keepdims=True)
    cached_w = (cached_exp / total * value_pos[None, None, :, None, :]).astype(jnp.bfloat16)
    own_w = (own_exp / total).astype(jnp.bfloat16)
    mixed = jnp.einsum(
        "btgql,lgd->btgqd", cached_w, rows_of_values, preferred_element_type=jnp.float32
    )
    mixed = mixed + jnp.einsum(
        "btgqs,bsgd->btgqd", own_w, fresh_values, preferred_element_type=jnp.float32
    )
    mixed = mixed.reshape(beam_total, draft_tokens, QUERY_HEADS * HEAD_SIZE)
    return (mixed * jax.nn.sigmoid(gate_rows.astype(jnp.float32))).astype(jnp.bfloat16)


def expert_kernel(
    n, x_ref, gate_ref, up_ref, down_ref, out_ref,
    rows_in, part, core_in, y_in, z_in,
    z_send, z_recv, y_send, y_recv, c_send, c_recv,
    core_send, core_recv, fold_send, fold_recv, last_send, last_recv, own_sem,
):
    deep = n // 4
    width = out_ref.shape[1]
    count = out_ref.shape[0]
    me = lax.axis_index("ep")
    c = lax.rem(me, 2)
    y = lax.rem(me // 2, 2)
    z = me // 4

    def at(zz, yy, cc):
        return (zz * 2 + yy) * 2 + cc

    other = at(z, y, 1 - c)
    across = at(z, 1 - y, c)
    up_z = [lax.rem(z + k, deep) for k in range(deep)]
    down_z = [lax.rem(z + deep - k, deep) for k in range(deep)]
    peers = [other, across] + [at(up_z[k], y, c) for k in range(1, deep)]
    barrier = pltpu.get_barrier_semaphore()
    for peer in peers:
        pl.semaphore_signal(barrier, inc=1, device_id={"ep": peer}, device_id_type=MESH)
    pl.semaphore_wait(barrier, len(peers))

    def send(src, dst, s_sem, r_sem, peer):
        copy = pltpu.make_async_remote_copy(
            src_ref=src, dst_ref=dst, send_sem=s_sem, recv_sem=r_sem,
            device_id={"ep": peer}, device_id_type=MESH,
        )
        copy.start()
        return copy

    own = pltpu.make_async_copy(x_ref, rows_in.at[me], own_sem)
    own.start()
    z_copies = {}
    y_copies = {0: send(x_ref, rows_in.at[me], y_send.at[0], y_recv.at[0], across)}
    for k in range(1, deep):
        z_copies[k] = send(x_ref, rows_in.at[me], z_send.at[k], z_recv.at[k], at(up_z[k], y, c))
    c_copies = {(0, 0): send(x_ref, rows_in.at[me], c_send.at[0], c_recv.at[0], other)}
    core_copies, fold_copies, last_copies = {}, {}, {}
    lanes = lax.broadcasted_iota(jnp.int32, (4 * count, MIX_COLUMNS), 1)
    picked = (lanes == me) | (lanes == me + n)

    def stage(k):
        z_copies[k].wait_recv()
        block = at(down_z[k], y, c)
        y_copies[k] = send(rows_in.at[block], rows_in.at[block], y_send.at[k], y_recv.at[k], across)
        c_copies[k, 0] = send(
            rows_in.at[block], rows_in.at[block], c_send.at[2 * k], c_recv.at[2 * k], other
        )

    def fold_y(k):
        y_here = at(down_z[k], y, c)
        fold_copies[k].wait_recv()
        part[y_here] = (
            part[y_here].astype(jnp.float32) + y_in[k].astype(jnp.float32)
        ).astype(jnp.bfloat16)
        if k:
            last_copies[k] = send(
                part.at[y_here], z_in.at[k], last_send.at[k], last_recv.at[k], y_here
            )

    for k in range(deep):
        y_copies[k].wait_recv()
        block = at(down_z[k], 1 - y, c)
        c_copies[k, 1] = send(
            rows_in.at[block], rows_in.at[block], c_send.at[2 * k + 1], c_recv.at[2 * k + 1], other
        )
        if k + 1 < deep:
            stage(k + 1)
        if k == 0:
            own.wait()
        c_copies[k, 0].wait_recv()
        c_copies[k, 1].wait_recv()
        first = pl.multiple_of(down_z[k] * 4, 4)
        rows = rows_in[pl.ds(first, 4)].reshape(4 * count, -1)
        mix = jnp.sum(
            jnp.where(picked, rows[:, width:].astype(jnp.float32), 0.0), axis=1, keepdims=True
        )
        rows = rows[:, :width]
        gate_val = jnp.dot(rows, gate_ref[...], preferred_element_type=jnp.float32)
        up_val = jnp.dot(rows, up_ref[...], preferred_element_type=jnp.float32)
        inner = (gate_val * jax.nn.sigmoid(gate_val) * up_val).astype(jnp.bfloat16)
        made = jnp.dot(inner, down_ref[...], preferred_element_type=jnp.float32)
        part[pl.ds(first, 4)] = (made * mix).astype(jnp.bfloat16).reshape(4, count, width)
        for yy in range(2):
            core_copies[k, yy] = send(
                part.at[at(down_z[k], yy, 1 - c)], core_in.at[2 * k + yy],
                core_send.at[2 * k + yy], core_recv.at[2 * k + yy], other,
            )
        for yy in range(2):
            core_copies[k, yy].wait_recv()
            here = at(down_z[k], yy, c)
            part[here] = (
                part[here].astype(jnp.float32) + core_in[2 * k + yy].astype(jnp.float32)
            ).astype(jnp.bfloat16)
        fold_copies[k] = send(
            part.at[at(down_z[k], 1 - y, c)], y_in.at[k], fold_send.at[k], fold_recv.at[k], across
        )
        if k:
            fold_y(k - 1)
    fold_y(deep - 1)
    total = part[me].astype(jnp.float32)
    for k in range(1, deep):
        last_copies[k].wait_recv()
        total = total + z_in[k].astype(jnp.float32)
    out_ref[...] = total.astype(jnp.bfloat16)
    for group in (z_copies, y_copies, c_copies, core_copies, fold_copies, last_copies):
        for copy in group.values():
            copy.wait_send()


def routed_experts(packed, gate_w, up_w, down_w, n):
    count = packed.shape[0]
    width = down_w.shape[1]
    deep = n // 4
    dma = pltpu.SemaphoreType.DMA
    return pl.pallas_call(
        functools.partial(expert_kernel, n),
        out_shape=jax.ShapeDtypeStruct((count, width), jnp.bfloat16),
        in_specs=[pl.BlockSpec(memory_space=pltpu.VMEM)] * 4,
        out_specs=pl.BlockSpec(memory_space=pltpu.VMEM),
        scratch_shapes=[
            pltpu.VMEM((n, count, packed.shape[1]), jnp.bfloat16),
            pltpu.VMEM((n, count, width), jnp.bfloat16),
            pltpu.VMEM((2 * deep, count, width), jnp.bfloat16),
            pltpu.VMEM((deep, count, width), jnp.bfloat16),
            pltpu.VMEM((deep, count, width), jnp.bfloat16),
            dma((deep,)), dma((deep,)), dma((deep,)), dma((deep,)),
            dma((2 * deep,)), dma((2 * deep,)), dma((2 * deep,)), dma((2 * deep,)),
            dma((deep,)), dma((deep,)), dma((deep,)), dma((deep,)), dma,
        ],
        compiler_params=pltpu.CompilerParams(
            collective_id=1, has_side_effects=True, vmem_limit_bytes=50 * 1024 * 1024
        ),
    )(packed, gate_w, up_w, down_w)


def normalize(vectors):
    return vectors * lax.rsqrt(jnp.sum(vectors * vectors, axis=-1, keepdims=True) + norm_eps)


def on_device(
    page_key_value_codes,
    page_key_scales,
    page_value_scales,
    block_table,
    prompt_lengths,
    decode_owner,
    prefill_states,
    att_query,
    att_gate,
    draft_keys_values,
    out_weight,
    residual,
    norm_gain,
    router_weight,
    expert_routes,
    gate_weight,
    up_weight,
    down_weight,
    gdn_qk,
    gdn_v,
    gdn_decay,
    gdn_beta,
):
    devices = lax.axis_size("ep")
    device_id = lax.axis_index("ep")
    labels = jnp.arange(devices, dtype=jnp.int32)
    matches = (decode_owner[:, None] == labels[None, :]).astype(jnp.int32)
    inverse = jnp.sum(labels[:, None] * matches, axis=0)
    page_ids = block_table[inverse]
    scales = jnp.concatenate(
        [page_key_scales[page_ids], page_value_scales[page_ids]], axis=-1
    ).reshape(devices, 1, -1)
    states = prefill_states[inverse].reshape(devices, -1, DK)
    scales = jnp.pad(scales, ((0, 0), (0, 15), (0, DK - scales.shape[2])))
    with_scales = lax.all_to_all(
        jnp.concatenate([states, scales], axis=1), "ep", split_axis=0, concat_axis=0, tiled=True
    )
    state_rows = states.shape[1]
    state_input = with_scales[:, :state_rows].reshape(-1, DK, DK)
    scale_input = with_scales[:, state_rows, : page_ids.shape[1] * 2 * KEY_VALUE_HEADS].reshape(
        -1, 2 * KEY_VALUE_HEADS
    )
    codes_input = lax.all_to_all(
        page_key_value_codes[page_ids], "ep", split_axis=0, concat_axis=0, tiled=True
    )
    prompt_id = inverse[device_id]
    length = prompt_lengths[prompt_id]
    codes_by_row = codes_input.reshape(-1, codes_input.shape[-1])
    scale_of_key = scale_input[:, :KEY_VALUE_HEADS]
    scale_of_value = scale_input[:, KEY_VALUE_HEADS:]
    gated_out = attend_prompt(
        att_query, att_gate, draft_keys_values, codes_by_row, scale_of_key, scale_of_value, length
    )
    beam_total = att_query.shape[0]
    draft_tokens = att_query.shape[1]
    row_count = beam_total * draft_tokens
    attn_mix = jnp.dot(
        gated_out.reshape(row_count, -1), out_weight, preferred_element_type=jnp.float32
    ).astype(jnp.bfloat16)
    hidden = residual.astype(jnp.float32).reshape(row_count, -1) + attn_mix.astype(jnp.float32)
    normed = (
        hidden
        * lax.rsqrt(jnp.mean(hidden * hidden, axis=-1, keepdims=True) + norm_eps)
        * norm_gain.astype(jnp.float32)
    ).astype(jnp.bfloat16)
    logits = jnp.dot(normed, router_weight, preferred_element_type=jnp.float32)
    routes = expert_routes.reshape(row_count, -1)
    experts = router_weight.shape[1]
    named = jnp.any(
        routes[:, :, None] == jnp.arange(experts, dtype=jnp.int32)[None, None, :], axis=1
    )
    mixing = jax.nn.softmax(jnp.where(named, logits, -jnp.inf), axis=-1)
    coarse = lax.reduce_precision(mixing, 8, 7)
    fine = mixing - coarse
    packed = jnp.concatenate(
        [
            normed,
            coarse.astype(jnp.bfloat16),
            fine.astype(jnp.bfloat16),
            jnp.zeros((row_count, MIX_COLUMNS - 2 * experts), jnp.bfloat16),
        ],
        axis=1,
    )
    moe_out = routed_experts(packed, gate_weight[0], up_weight[0], down_weight[0], devices)
    current_state = state_input.astype(jnp.float32)
    head_count = current_state.shape[0]
    half_width = gdn_qk.shape[-1] // 2
    key_heads = half_width // DK
    head_pairs = head_count // key_heads
    qk_values = gdn_qk.astype(jnp.float32)
    query_vec = normalize(
        qk_values[..., :half_width].reshape(beam_total, draft_tokens, key_heads, DK)
    ) * DK ** (-0.5)
    key_vec = normalize(
        qk_values[..., half_width:].reshape(beam_total, draft_tokens, key_heads, DK)
    )
    query_vec = jnp.repeat(query_vec, head_pairs, axis=2)
    key_vec = jnp.repeat(key_vec, head_pairs, axis=2)
    probe_queries = jnp.concatenate([key_vec, query_vec], axis=1)
    cache_images = jnp.einsum(
        "ijr,flij->flir", current_state, probe_queries, precision=lax.Precision.HIGHEST
    )
    inner_prod = jnp.einsum(
        "bthk,bnhk->btnh", key_vec, probe_queries, precision=lax.Precision.HIGHEST
    )
    value_vec = gdn_v.astype(jnp.float32).reshape(beam_total, draft_tokens, head_count, -1)
    outputs = []
    for draft_idx in range(draft_tokens):
        decay_now = gdn_decay[:, draft_idx][:, None, :, None]
        write_rate = gdn_beta[:, draft_idx][:, None, :, None]
        keyed_image = cache_images[:, draft_idx][:, None]
        along_key = inner_prod[:, draft_idx][..., None]
        cache_images = (
            decay_now * cache_images
            + write_rate * (value_vec[:, draft_idx][:, None] - decay_now * keyed_image) * along_key
        )
        outputs.append(cache_images[:, draft_tokens + draft_idx])
    gdn_out = jnp.stack(outputs, axis=1).reshape(beam_total, draft_tokens, -1).astype(jnp.bfloat16)
    return (
        attn_mix.reshape(beam_total, draft_tokens, -1),
        moe_out.reshape(beam_total, draft_tokens, -1),
        gdn_out,
    )


def solution(mesh):
    placed = (
        P(("grp", "ep"), None, None),
        P(("grp", "ep"), None),
        P(("grp", "ep"), None),
        P("grp", "ep"),
        P("grp"),
        P("grp"),
        P("grp", "ep", None, None),
        P(("grp", "ep"), None, None),
        P(("grp", "ep"), None, None),
        P(("grp", "ep"), None, None),
        P(),
        P(("grp", "ep"), None, None),
        P(),
        P(),
        P(("grp", "ep"), None, None),
        P("ep", None, None),
        P("ep", None, None),
        P("ep", None, None),
        P(("grp", "ep"), None, None),
        P(("grp", "ep"), None, None),
        P(("grp", "ep"), None, None),
        P(("grp", "ep"), None, None),
    )
    return jax.shard_map(
        on_device,
        mesh=mesh,
        in_specs=placed,
        out_specs=(
            P(("grp", "ep"), None, None),
            P(("grp", "ep"), None, None),
            P(("grp", "ep"), None, None),
        ),
        check_vma=False,
    )
```

```python
import functools

import jax
import jax.numpy as jnp
from jax import lax
from jax.experimental import pallas as pl
from jax.experimental.pallas import tpu as pltpu
from jax.sharding import PartitionSpec as P

MESH = pl.DeviceIdType.MESH
MIX_COLUMNS = 128

QUERY_HEADS = 8
KEY_VALUE_HEADS = 2
HEAD_SIZE = 256
DK = 128
PAGE_POSITIONS = 32
DRAFTS = 4


norm_eps = 1e-06
masked_score = -1e30


def attend_kernel(
    experts, n, q_ref, gate_ref, fresh_ref, codes_src, scales_src, live_ref, out_w_hbm,
    residual_ref, gain_ref, router_ref, named_ref, attn_ref, packed_ref,
    gated, codes_in, scales_in, out_w_ref, send_sem, recv_sem, scale_send, scale_recv, own_sem,
):
    me = lax.axis_index("ep")
    barrier = pltpu.get_barrier_semaphore()
    peers = [lax.rem(me + k, n) for k in range(n)]
    for k in range(1, n):
        pl.semaphore_signal(barrier, inc=1, device_id={"ep": peers[k]}, device_id_type=MESH)
    pl.semaphore_wait(barrier, n - 1)
    copies = []
    for k in range(1, n):
        for src, dst, s_sem, r_sem in (
            (scales_src, scales_in, scale_send, scale_recv),
            (codes_src, codes_in, send_sem, recv_sem),
        ):
            copy = pltpu.make_async_remote_copy(
                src_ref=src.at[peers[k]], dst_ref=dst.at[me], send_sem=s_sem.at[k],
                recv_sem=r_sem.at[k], device_id={"ep": peers[k]}, device_id_type=MESH,
            )
            copy.start()
            copies.append(copy)
    local = [
        pltpu.make_async_copy(codes_src.at[me], codes_in.at[me], own_sem.at[0]),
        pltpu.make_async_copy(scales_src.at[me], scales_in.at[me], own_sem.at[1]),
        pltpu.make_async_copy(out_w_hbm, out_w_ref, own_sem.at[2]),
    ]
    for copy in local:
        copy.start()
    for copy in copies + local:
        copy.wait()
    scales = jnp.concatenate(
        [
            scales_in[2 * i].astype(jnp.float32) + scales_in[2 * i + 1].astype(jnp.float32)
            for i in range(n // 2)
        ],
        axis=1,
    )
    length = live_ref.shape[1]

    def codes(columns):
        return codes_in[:, :, columns].reshape(length, HEAD_SIZE)

    count = q_ref.shape[0]
    groups = QUERY_HEADS // KEY_VALUE_HEADS
    half = KEY_VALUE_HEADS * HEAD_SIZE
    factor = HEAD_SIZE ** (-0.5)
    across_last = (((1,), (1,)), ((), ()))
    row = lax.broadcasted_iota(jnp.int32, (groups * count, count), 0) % count
    column = lax.broadcasted_iota(jnp.int32, (groups * count, count), 1)
    causal = (row // DRAFTS == column // DRAFTS) & (column <= row)
    live = live_ref[...] > 0.0
    for g in range(KEY_VALUE_HEADS):
        q = jnp.concatenate(
            [
                q_ref[:, (g * groups + i) * HEAD_SIZE : (g * groups + i + 1) * HEAD_SIZE]
                for i in range(groups)
            ],
            axis=0,
        )
        keys = slice(g * HEAD_SIZE, (g + 1) * HEAD_SIZE)
        values = slice(half + g * HEAD_SIZE, half + (g + 1) * HEAD_SIZE)
        cached = lax.dot_general(
            q, codes(keys), across_last, preferred_element_type=jnp.float32
        )
        cached = jnp.where(live, cached * scales[g : g + 1] * factor, masked_score)
        own = lax.dot_general(
            q, fresh_ref[:, keys], across_last, preferred_element_type=jnp.float32
        )
        own = jnp.where(causal, own * factor, masked_score)
        top = jnp.maximum(
            jnp.max(cached, axis=1, keepdims=True), jnp.max(own, axis=1, keepdims=True)
        )
        cached = jnp.exp(cached - top)
        own = jnp.exp(own - top)
        scale = 1.0 / (
            jnp.sum(cached, axis=1, keepdims=True) + jnp.sum(own, axis=1, keepdims=True)
        )
        cached = (cached * scale * scales[KEY_VALUE_HEADS + g : KEY_VALUE_HEADS + g + 1]).astype(jnp.bfloat16)
        own = (own * scale).astype(jnp.bfloat16)
        mixed = jnp.dot(cached, codes(values), preferred_element_type=jnp.float32)
        mixed = mixed + jnp.dot(own, fresh_ref[:, values], preferred_element_type=jnp.float32)
        for i in range(groups):
            head = slice((g * groups + i) * HEAD_SIZE, (g * groups + i + 1) * HEAD_SIZE)
            gate = jax.nn.sigmoid(gate_ref[:, head].astype(jnp.float32))
            gated[:, head] = (mixed[i * count : (i + 1) * count] * gate).astype(jnp.bfloat16)
    attn = jnp.dot(gated[...], out_w_ref[...], preferred_element_type=jnp.float32).astype(
        jnp.bfloat16
    )
    attn_ref[...] = attn
    hidden = residual_ref[...].astype(jnp.float32) + attn.astype(jnp.float32)
    normed = (
        hidden
        * lax.rsqrt(jnp.mean(hidden * hidden, axis=1, keepdims=True) + norm_eps)
        * gain_ref[...]
    ).astype(jnp.bfloat16)
    width = normed.shape[1]
    packed_ref[:, :width] = normed
    logits = jnp.dot(normed, router_ref[...], preferred_element_type=jnp.float32)
    named = named_ref[...] > 0.0
    logits = jnp.where(named, logits, masked_score)
    raised = jnp.where(named, jnp.exp(logits - jnp.max(logits, axis=1, keepdims=True)), 0.0)
    lane = lax.broadcasted_iota(jnp.int32, raised.shape, 1)
    mixing = raised / jnp.sum(jnp.where(lane < experts, raised, 0.0), axis=1, keepdims=True)
    coarse = mixing.astype(jnp.bfloat16)
    fine = (mixing - coarse.astype(jnp.float32)).astype(jnp.bfloat16)
    packed_ref[:, width:] = jnp.where(
        lane < experts, coarse.astype(jnp.float32), fine.astype(jnp.float32)
    ).astype(jnp.bfloat16)


def attend(experts, *operands):
    count, width = operands[0].shape
    whole = pl.BlockSpec(memory_space=pltpu.VMEM)
    specs = [whole] * len(operands)
    specs[3] = specs[6] = pl.BlockSpec(memory_space=pl.ANY)
    n = operands[3].shape[0]
    dma = pltpu.SemaphoreType.DMA
    return pl.pallas_call(
        functools.partial(attend_kernel, experts, n),
        out_shape=(
            jax.ShapeDtypeStruct((count, width), jnp.bfloat16),
            jax.ShapeDtypeStruct((count, width + MIX_COLUMNS), jnp.bfloat16),
        ),
        in_specs=specs,
        out_specs=(whole, whole),
        scratch_shapes=[
            pltpu.VMEM((count, width), jnp.bfloat16),
            pltpu.VMEM(operands[3].shape, jnp.bfloat16),
            pltpu.VMEM(operands[4].shape, jnp.bfloat16),
            pltpu.VMEM(operands[6].shape, jnp.bfloat16),
            dma((n,)), dma((n,)), dma((n,)), dma((n,)), dma((3,)),
        ],
        compiler_params=pltpu.CompilerParams(
            collective_id=0, has_side_effects=True, vmem_limit_bytes=50 * 1024 * 1024
        ),
    )(*operands)


def delta_heads(qk_ref, v_ref, decay_ref, beta_ref, state_ref, out_ref, first, last):
    beams = qk_ref.shape[0] // DRAFTS
    half = qk_ref.shape[1] // 2
    local = state_ref.shape[1]
    heads = state_ref.shape[0] * local
    pairs = heads // (half // DK)
    lane = lax.broadcasted_iota(jnp.int32, decay_ref.shape, 1)

    def rows(x, t):
        return x[t * beams : (t + 1) * beams]

    def product(x, y):
        return jnp.sum(x * y, axis=1, keepdims=True)

    def one(j, carry):
        start = pl.multiple_of(j * DK, DK)
        key_start = pl.multiple_of(half + j * DK, DK)
        q = qk_ref[:, pl.ds(start, DK)].astype(jnp.float32)
        k = qk_ref[:, pl.ds(key_start, DK)].astype(jnp.float32)
        q = q * lax.rsqrt(product(q, q) + norm_eps) * DK ** (-0.5)
        k = k * lax.rsqrt(product(k, k) + norm_eps)
        probes = jnp.concatenate([k, q], axis=0)
        coarse = probes.astype(jnp.bfloat16)
        fine = (probes - coarse.astype(jnp.float32)).astype(jnp.bfloat16)
        probes = jnp.concatenate([coarse, fine], axis=0)
        half_rows = 2 * DRAFTS * beams
        along_key = {
            (s, t): product(rows(k, s), rows(k, t)) for t in range(DRAFTS) for s in range(t)
        }
        along_query = {
            (s, t): product(rows(k, s), rows(q, t)) for t in range(DRAFTS) for s in range(t + 1)
        }
        for part in range(pairs):
            head = j * pairs + part
            images = jnp.dot(
                probes, state_ref[head // local, head % local], preferred_element_type=jnp.float32)
            images = images[:half_rows] + images[half_rows:]
            decay = jnp.sum(jnp.where(lane == head, decay_ref[...], 0.0), axis=1, keepdims=True)
            beta = jnp.sum(jnp.where(lane == head, beta_ref[...], 0.0), axis=1, keepdims=True)
            columns = pl.ds(pl.multiple_of(head * DK, DK), DK)
            v = v_ref[:, columns].astype(jnp.float32)
            kept = None
            weights, writes = [], []
            for t in range(DRAFTS):
                seen = rows(images, t) if kept is None else kept * rows(images, t)
                for s in range(t):
                    seen = seen + (weights[s] * along_key[s, t]) * writes[s]
                now = rows(decay, t)
                writes.append(rows(v, t) - now * seen)
                kept = now if kept is None else kept * now
                weights = [now * w for w in weights] + [rows(beta, t)]
                got = kept * rows(images, DRAFTS + t)
                for s in range(t + 1):
                    got = got + (weights[s] * along_query[s, t]) * writes[s]
                out_ref[t * beams : (t + 1) * beams, columns] = got.astype(jnp.bfloat16)
        return carry

    lax.fori_loop(first, last, one, 0)


def expert_kernel(
    n, x_ref, gate_hbm, up_hbm, down_hbm, qk_hbm, v_hbm, decay_ref, beta_ref, state_src,
    out_ref, delta_ref, rows_in, part, core_in, y_in, z_in,
    z_send, z_recv, y_send, y_recv, c_send, c_recv,
    core_send, core_recv, fold_send, fold_recv, last_send, last_recv, own_sem,
    gate_ref, up_ref, down_ref, qk_ref, v_ref, state_ref, state_send, state_recv,
):
    deep = n // 4
    width = out_ref.shape[1]
    count = out_ref.shape[0]
    me = lax.axis_index("ep")
    c = lax.rem(me, 2)
    y = lax.rem(me // 2, 2)
    z = me // 4

    def at(zz, yy, cc):
        return (zz * 2 + yy) * 2 + cc

    other = at(z, y, 1 - c)
    across = at(z, 1 - y, c)
    near = jnp.minimum(z, deep - 1 - z)
    turn = [z]
    for k in range(1, deep):
        close = z - (k + 1) // 2 if k % 2 else z + k // 2
        far = jnp.where(z > near, z - (k - near), z + (k - near))
        turn.append(jnp.where(k <= 2 * near, close, far))
    peers = [lax.rem(me + k, n) for k in range(1, n)]
    barrier = pltpu.get_barrier_semaphore()
    for peer in peers:
        pl.semaphore_signal(barrier, inc=1, device_id={"ep": peer}, device_id_type=MESH)
    pl.semaphore_wait(barrier, len(peers))

    def send(src, dst, s_sem, r_sem, peer):
        copy = pltpu.make_async_remote_copy(
            src_ref=src, dst_ref=dst, send_sem=s_sem, recv_sem=r_sem,
            device_id={"ep": peer}, device_id_type=MESH,
        )
        copy.start()
        return copy

    local = [
        pltpu.make_async_copy(src, dst, own_sem.at[i])
        for i, (src, dst) in enumerate((
            (x_ref, rows_in.at[me]), (gate_hbm, gate_ref), (up_hbm, up_ref),
            (down_hbm, down_ref), (qk_hbm, qk_ref), (v_hbm, v_ref),
            (state_src.at[me], state_ref.at[me]),
        ))
    ]
    y_copies = {0: send(x_ref, rows_in.at[me], y_send.at[0], y_recv.at[0], across)}

    def pass_on(src, block, origin, k, target):
        return pltpu.make_async_remote_copy(
            src_ref=src, dst_ref=rows_in.at[block], send_sem=z_send.at[k],
            recv_sem=z_recv.at[origin], device_id={"ep": at(target, y, c)}, device_id_type=MESH,
        )

    above, below = lax.rem(z + 1, deep), lax.rem(z + deep - 1, deep)

    @pl.when(z + 1 < deep)
    def _():
        pass_on(x_ref, me, z, 0, above).start()

    @pl.when(z > 0)
    def _():
        pass_on(x_ref, me, z, deep, below).start()

    c_copies = {(0, 0): send(x_ref, rows_in.at[me], c_send.at[0], c_recv.at[0], other)}
    for copy in local:
        copy.start()
    state_copies = {
        k: send(
            state_src.at[peers[k - 1]], state_ref.at[me], state_send.at[k], state_recv.at[k],
            peers[k - 1],
        )
        for k in range(1, n)
    }
    core_copies, fold_copies, last_copies = {}, {}, {}
    lanes = lax.broadcasted_iota(jnp.int32, (4 * count, MIX_COLUMNS), 1)
    picked = (lanes == me) | (lanes == me + n)

    def onward(k):
        block = at(turn[k], y, c)
        target = jnp.where(turn[k] < z, above, below)
        goes = jnp.where(turn[k] < z, z + 1 < deep, z > 0)
        return goes, pass_on(rows_in.at[block], block, turn[k], k, target)

    def stage(k):
        block = at(turn[k], y, c)
        goes, copy = onward(k)
        copy.wait_recv()

        @pl.when(goes)
        def _():
            copy.start()

        y_copies[k] = send(rows_in.at[block], rows_in.at[block], y_send.at[k], y_recv.at[k], across)
        c_copies[k, 0] = send(
            rows_in.at[block], rows_in.at[block], c_send.at[2 * k], c_recv.at[2 * k], other
        )

    key_heads = qk_ref.shape[1] // (2 * DK)

    def delta(first, last):
        delta_heads(
            qk_ref, v_ref, decay_ref, beta_ref, state_ref, delta_ref, first, last
        )

    def fold_y(k):
        y_here = at(turn[k], y, c)
        fold_copies[k].wait_recv()
        part[y_here] = (
            part[y_here].astype(jnp.float32) + y_in[k].astype(jnp.float32)
        ).astype(jnp.bfloat16)
        if k:
            last_copies[k] = send(
                part.at[y_here], z_in.at[z], last_send.at[k], last_recv.at[z], y_here
            )

    for k in range(deep):
        y_copies[k].wait_recv()
        block = at(turn[k], 1 - y, c)
        c_copies[k, 1] = send(
            rows_in.at[block], rows_in.at[block], c_send.at[2 * k + 1], c_recv.at[2 * k + 1], other
        )
        if k + 1 < deep:
            stage(k + 1)
        if k == 0:
            for copy in local:
                copy.wait()
        c_copies[k, 0].wait_recv()
        c_copies[k, 1].wait_recv()
        first = pl.multiple_of(turn[k] * 4, 4)
        rows = rows_in[pl.ds(first, 4)].reshape(4 * count, -1)
        mix = jnp.sum(
            jnp.where(picked, rows[:, width:].astype(jnp.float32), 0.0), axis=1, keepdims=True
        )
        rows = rows[:, :width]
        gate_val = jnp.dot(rows, gate_ref[...], preferred_element_type=jnp.float32)
        up_val = jnp.dot(rows, up_ref[...], preferred_element_type=jnp.float32)
        inner = (gate_val * jax.nn.sigmoid(gate_val) * up_val).astype(jnp.bfloat16)
        made = jnp.dot(inner, down_ref[...], preferred_element_type=jnp.float32)
        part[pl.ds(first, 4)] = (made * mix).astype(jnp.bfloat16).reshape(4, count, width)
        for yy in range(2):
            core_copies[k, yy] = send(
                part.at[at(turn[k], yy, 1 - c)], core_in.at[2 * k + yy],
                core_send.at[2 * k + yy], core_recv.at[2 * k + yy], other,
            )
        for yy in range(2):
            core_copies[k, yy].wait_recv()
            here = at(turn[k], yy, c)
            part[here] = (
                part[here].astype(jnp.float32) + core_in[2 * k + yy].astype(jnp.float32)
            ).astype(jnp.bfloat16)
        fold_copies[k] = send(
            part.at[at(turn[k], 1 - y, c)], y_in.at[k], fold_send.at[k], fold_recv.at[k], across
        )
        if k:
            fold_y(k - 1)
    for copy in state_copies.values():
        copy.wait_recv()
    delta(0, key_heads // 2)
    fold_y(deep - 1)
    delta(key_heads // 2, key_heads)
    total = part[me].astype(jnp.float32)
    for k in range(1, deep):
        pltpu.make_async_remote_copy(
            src_ref=part.at[me], dst_ref=z_in.at[turn[k]], send_sem=last_send.at[k],
            recv_sem=last_recv.at[turn[k]], device_id={"ep": other}, device_id_type=MESH,
        ).wait_recv()
        total = total + z_in[turn[k]].astype(jnp.float32)
    out_ref[...] = total.astype(jnp.bfloat16)
    @pl.when(z + 1 < deep)
    def _():
        pass_on(x_ref, me, z, 0, above).wait_send()

    @pl.when(z > 0)
    def _():
        pass_on(x_ref, me, z, deep, below).wait_send()

    for k in range(1, deep):
        goes, copy = onward(k)

        @pl.when(goes)
        def _():
            copy.wait_send()

    for group in (state_copies, y_copies, c_copies, core_copies, fold_copies, last_copies):
        for copy in group.values():
            copy.wait_send()


def routed_experts(packed, gate_w, up_w, down_w, qk, v, decay, beta, states, n):
    count = packed.shape[0]
    width = down_w.shape[1]
    deep = n // 4
    dma = pltpu.SemaphoreType.DMA
    return pl.pallas_call(
        functools.partial(expert_kernel, n),
        out_shape=(
            jax.ShapeDtypeStruct((count, width), jnp.bfloat16),
            jax.ShapeDtypeStruct(v.shape, jnp.bfloat16),
        ),
        in_specs=[
            pl.BlockSpec(memory_space=pl.ANY if i in (1, 2, 3, 4, 5, 8) else pltpu.VMEM)
            for i in range(9)
        ],
        out_specs=(pl.BlockSpec(memory_space=pltpu.VMEM), pl.BlockSpec(memory_space=pltpu.VMEM)),
        scratch_shapes=[
            pltpu.VMEM((n, count, packed.shape[1]), jnp.bfloat16),
            pltpu.VMEM((n, count, width), jnp.bfloat16),
            pltpu.VMEM((2 * deep, count, width), jnp.bfloat16),
            pltpu.VMEM((deep, count, width), jnp.bfloat16),
            pltpu.VMEM((deep, count, width), jnp.bfloat16),
            dma((deep + 1,)), dma((deep,)), dma((deep,)), dma((deep,)),
            dma((2 * deep,)), dma((2 * deep,)), dma((2 * deep,)), dma((2 * deep,)),
            dma((deep,)), dma((deep,)), dma((deep,)), dma((deep,)), dma((7,)),
            *(pltpu.VMEM(x.shape, jnp.bfloat16) for x in (gate_w, up_w, down_w, qk, v, states)),
            dma((n,)), dma((n,)),
        ],
        compiler_params=pltpu.CompilerParams(
            collective_id=1, has_side_effects=True, vmem_limit_bytes=50 * 1024 * 1024
        ),
    )(packed, gate_w, up_w, down_w, qk, v, decay, beta, states)


def on_device(
    page_key_value_codes,
    page_key_scales,
    page_value_scales,
    block_table,
    prompt_lengths,
    decode_owner,
    prefill_states,
    att_query,
    att_gate,
    draft_keys_values,
    out_weight,
    residual,
    norm_gain,
    router_weight,
    expert_routes,
    gate_weight,
    up_weight,
    down_weight,
    gdn_qk,
    gdn_v,
    gdn_decay,
    gdn_beta,
):
    devices = lax.axis_size("ep")
    device_id = lax.axis_index("ep")
    labels = jnp.arange(devices, dtype=jnp.int32)
    matches = (decode_owner[:, None] == labels[None, :]).astype(jnp.int32)
    inverse = jnp.sum(labels[:, None] * matches, axis=0)
    page_ids = block_table[inverse]
    scales = jnp.concatenate([page_key_scales[page_ids], page_value_scales[page_ids]], axis=-1)
    scales = jnp.repeat(scales, PAGE_POSITIONS, axis=1).transpose(0, 2, 1)
    scales = jnp.pad(scales, ((0, 0), (0, 16 - scales.shape[1]), (0, 0)))
    blank = jnp.zeros_like(scales)
    scales = jnp.where(
        device_id % 2 == 0,
        jnp.concatenate([scales, blank], axis=2),
        jnp.concatenate([blank, scales], axis=2),
    )
    codes = page_key_value_codes[page_ids]
    codes = codes.reshape(devices, -1, codes.shape[-1])
    states = prefill_states[inverse]
    length = prompt_lengths[inverse[device_id]]
    live = (jnp.arange(devices * codes.shape[1], dtype=jnp.int32) < length).astype(jnp.float32)[None]
    beam_total, draft_tokens, width = att_query.shape
    row_count = beam_total * draft_tokens

    def flat(x):
        return x.reshape(row_count, -1)

    def by_draft(x):
        return x.transpose(1, 0, 2).reshape(row_count, -1)

    experts = router_weight.shape[1]
    spare = MIX_COLUMNS - 2 * experts
    router = jnp.concatenate([router_weight, router_weight], axis=1)
    router = jnp.pad(router, ((0, 0), (0, spare)))
    named = jnp.any(
        flat(expert_routes)[:, :, None] == jnp.arange(experts, dtype=jnp.int32)[None, None, :],
        axis=1,
    ).astype(jnp.float32)
    named = jnp.pad(jnp.concatenate([named, named], axis=1), ((0, 0), (0, spare)))
    attn_mix, packed = attend(
        experts,
        flat(att_query),
        flat(att_gate),
        flat(draft_keys_values),
        codes,
        scales,
        live,
        out_weight,
        flat(residual),
        norm_gain.astype(jnp.float32)[None],
        router,
        named,
    )
    moe_out, gdn_out = routed_experts(
        packed, gate_weight[0], up_weight[0], down_weight[0],
        by_draft(gdn_qk), by_draft(gdn_v), by_draft(gdn_decay), by_draft(gdn_beta), states, devices,
    )
    return (
        attn_mix.reshape(att_query.shape),
        moe_out.reshape(att_query.shape),
        gdn_out.reshape(draft_tokens, beam_total, -1).transpose(1, 0, 2),
    )


def solution(mesh):
    placed = (
        P(("grp", "ep"), None, None),
        P(("grp", "ep"), None),
        P(("grp", "ep"), None),
        P("grp", "ep"),
        P("grp"),
        P("grp"),
        P("grp", "ep", None, None),
        P(("grp", "ep"), None, None),
        P(("grp", "ep"), None, None),
        P(("grp", "ep"), None, None),
        P(),
        P(("grp", "ep"), None, None),
        P(),
        P(),
        P(("grp", "ep"), None, None),
        P("ep", None, None),
        P("ep", None, None),
        P("ep", None, None),
        P(("grp", "ep"), None, None),
        P(("grp", "ep"), None, None),
        P(("grp", "ep"), None, None),
        P(("grp", "ep"), None, None),
    )
    return jax.shard_map(
        on_device,
        mesh=mesh,
        in_specs=placed,
        out_specs=(
            P(("grp", "ep"), None, None),
            P(("grp", "ep"), None, None),
            P(("grp", "ep"), None, None),
        ),
        check_vma=False,
    )
```

```python
import functools

import jax
import jax.numpy as jnp
from jax import lax
from jax.experimental import pallas as pl
from jax.experimental.pallas import tpu as pltpu
from jax.sharding import PartitionSpec as P

MESH = pl.DeviceIdType.MESH
MIX_COLUMNS = 128

QUERY_HEADS = 8
KEY_VALUE_HEADS = 2
HEAD_SIZE = 256
DK = 128
PAGE_POSITIONS = 32
DRAFTS = 4


norm_eps = 1e-06
masked_score = -1e30


def attend_kernel(
    experts, n, q_ref, gate_ref, fresh_ref, codes_src, scales_src, live_ref, out_w_hbm,
    residual_ref, gain_ref, router_ref, named_ref, attn_ref, packed_ref,
    gated, codes_in, scales_in, out_w_ref, send_sem, recv_sem, scale_send, scale_recv, own_sem,
):
    me = lax.axis_index("ep")
    barrier = pltpu.get_barrier_semaphore()
    peers = [lax.rem(me + k, n) for k in range(n)]
    for k in range(1, n):
        pl.semaphore_signal(barrier, inc=1, device_id={"ep": peers[k]}, device_id_type=MESH)
    pl.semaphore_wait(barrier, n - 1)
    copies = []
    for k in range(1, n):
        for src, dst, s_sem, r_sem in (
            (scales_src, scales_in, scale_send, scale_recv),
            (codes_src, codes_in, send_sem, recv_sem),
        ):
            copy = pltpu.make_async_remote_copy(
                src_ref=src.at[peers[k]], dst_ref=dst.at[me], send_sem=s_sem.at[k],
                recv_sem=r_sem.at[k], device_id={"ep": peers[k]}, device_id_type=MESH,
            )
            copy.start()
            copies.append(copy)
    local = [
        pltpu.make_async_copy(codes_src.at[me], codes_in.at[me], own_sem.at[0]),
        pltpu.make_async_copy(scales_src.at[me], scales_in.at[me], own_sem.at[1]),
        pltpu.make_async_copy(out_w_hbm, out_w_ref, own_sem.at[2]),
    ]
    for copy in local:
        copy.start()
    for copy in copies + local:
        copy.wait()
    scales = jnp.concatenate(
        [
            scales_in[2 * i].astype(jnp.float32) + scales_in[2 * i + 1].astype(jnp.float32)
            for i in range(n // 2)
        ],
        axis=1,
    )
    length = live_ref.shape[1]

    def codes(columns):
        return codes_in[:, :, columns].reshape(length, HEAD_SIZE)

    count = q_ref.shape[0]
    groups = QUERY_HEADS // KEY_VALUE_HEADS
    half = KEY_VALUE_HEADS * HEAD_SIZE
    factor = HEAD_SIZE ** (-0.5)
    across_last = (((1,), (1,)), ((), ()))
    row = lax.broadcasted_iota(jnp.int32, (groups * count, count), 0) % count
    column = lax.broadcasted_iota(jnp.int32, (groups * count, count), 1)
    causal = (row // DRAFTS == column // DRAFTS) & (column <= row)
    live = live_ref[...] > 0.0
    for g in range(KEY_VALUE_HEADS):
        q = jnp.concatenate(
            [
                q_ref[:, (g * groups + i) * HEAD_SIZE : (g * groups + i + 1) * HEAD_SIZE]
                for i in range(groups)
            ],
            axis=0,
        )
        keys = slice(g * HEAD_SIZE, (g + 1) * HEAD_SIZE)
        values = slice(half + g * HEAD_SIZE, half + (g + 1) * HEAD_SIZE)
        cached = lax.dot_general(
            q, codes(keys), across_last, preferred_element_type=jnp.float32
        )
        cached = jnp.where(live, cached * scales[g : g + 1] * factor, masked_score)
        own = lax.dot_general(
            q, fresh_ref[:, keys], across_last, preferred_element_type=jnp.float32
        )
        own = jnp.where(causal, own * factor, masked_score)
        top = jnp.maximum(
            jnp.max(cached, axis=1, keepdims=True), jnp.max(own, axis=1, keepdims=True)
        )
        cached = jnp.exp(cached - top)
        own = jnp.exp(own - top)
        scale = 1.0 / (
            jnp.sum(cached, axis=1, keepdims=True) + jnp.sum(own, axis=1, keepdims=True)
        )
        cached = (cached * scale * scales[KEY_VALUE_HEADS + g : KEY_VALUE_HEADS + g + 1]).astype(jnp.bfloat16)
        own = (own * scale).astype(jnp.bfloat16)
        mixed = jnp.dot(cached, codes(values), preferred_element_type=jnp.float32)
        mixed = mixed + jnp.dot(own, fresh_ref[:, values], preferred_element_type=jnp.float32)
        for i in range(groups):
            head = slice((g * groups + i) * HEAD_SIZE, (g * groups + i + 1) * HEAD_SIZE)
            gate = jax.nn.sigmoid(gate_ref[:, head].astype(jnp.float32))
            gated[:, head] = (mixed[i * count : (i + 1) * count] * gate).astype(jnp.bfloat16)
    attn = jnp.dot(gated[...], out_w_ref[...], preferred_element_type=jnp.float32).astype(
        jnp.bfloat16
    )
    attn_ref[...] = attn
    hidden = residual_ref[...].astype(jnp.float32) + attn.astype(jnp.float32)
    normed = (
        hidden
        * lax.rsqrt(jnp.mean(hidden * hidden, axis=1, keepdims=True) + norm_eps)
        * gain_ref[...]
    ).astype(jnp.bfloat16)
    width = normed.shape[1]
    packed_ref[:, :width] = normed
    logits = jnp.dot(normed, router_ref[...], preferred_element_type=jnp.float32)
    named = named_ref[...] > 0.0
    logits = jnp.where(named, logits, masked_score)
    raised = jnp.where(named, jnp.exp(logits - jnp.max(logits, axis=1, keepdims=True)), 0.0)
    lane = lax.broadcasted_iota(jnp.int32, raised.shape, 1)
    mixing = raised / jnp.sum(jnp.where(lane < experts, raised, 0.0), axis=1, keepdims=True)
    coarse = mixing.astype(jnp.bfloat16)
    fine = (mixing - coarse.astype(jnp.float32)).astype(jnp.bfloat16)
    packed_ref[:, width:] = jnp.where(
        lane < experts, coarse.astype(jnp.float32), fine.astype(jnp.float32)
    ).astype(jnp.bfloat16)


def attend(experts, *operands):
    count, width = operands[0].shape
    whole = pl.BlockSpec(memory_space=pltpu.VMEM)
    specs = [whole] * len(operands)
    specs[3] = specs[6] = pl.BlockSpec(memory_space=pl.ANY)
    n = operands[3].shape[0]
    dma = pltpu.SemaphoreType.DMA
    return pl.pallas_call(
        functools.partial(attend_kernel, experts, n),
        out_shape=(
            jax.ShapeDtypeStruct((count, width), jnp.bfloat16),
            jax.ShapeDtypeStruct((count, width + MIX_COLUMNS), jnp.bfloat16),
        ),
        in_specs=specs,
        out_specs=(whole, whole),
        scratch_shapes=[
            pltpu.VMEM((count, width), jnp.bfloat16),
            pltpu.VMEM(operands[3].shape, jnp.bfloat16),
            pltpu.VMEM(operands[4].shape, jnp.bfloat16),
            pltpu.VMEM(operands[6].shape, jnp.bfloat16),
            dma((n,)), dma((n,)), dma((n,)), dma((n,)), dma((3,)),
        ],
        compiler_params=pltpu.CompilerParams(
            collective_id=0, has_side_effects=True, vmem_limit_bytes=50 * 1024 * 1024
        ),
    )(*operands)


def delta_heads(qk_ref, v_ref, decay_ref, beta_ref, state_ref, out_ref, first, last):
    beams = qk_ref.shape[0] // DRAFTS
    half = qk_ref.shape[1] // 2
    local = state_ref.shape[1]
    heads = state_ref.shape[0] * local
    pairs = heads // (half // DK)
    lane = lax.broadcasted_iota(jnp.int32, decay_ref.shape, 1)

    def rows(x, t):
        return x[t * beams : (t + 1) * beams]

    def product(x, y):
        return jnp.sum(x * y, axis=1, keepdims=True)

    def one(j, carry):
        start = pl.multiple_of(j * DK, DK)
        key_start = pl.multiple_of(half + j * DK, DK)
        q = qk_ref[:, pl.ds(start, DK)].astype(jnp.float32)
        k = qk_ref[:, pl.ds(key_start, DK)].astype(jnp.float32)
        q = q * lax.rsqrt(product(q, q) + norm_eps) * DK ** (-0.5)
        k = k * lax.rsqrt(product(k, k) + norm_eps)
        probes = jnp.concatenate([k, q], axis=0)
        coarse = probes.astype(jnp.bfloat16)
        fine = (probes - coarse.astype(jnp.float32)).astype(jnp.bfloat16)
        probes = jnp.concatenate([coarse, fine], axis=0)
        half_rows = 2 * DRAFTS * beams
        along_key = {
            (s, t): product(rows(k, s), rows(k, t)) for t in range(DRAFTS) for s in range(t)
        }
        along_query = {
            (s, t): product(rows(k, s), rows(q, t)) for t in range(DRAFTS) for s in range(t + 1)
        }
        for part in range(pairs):
            head = j * pairs + part
            images = jnp.dot(
                probes, state_ref[head // local, head % local], preferred_element_type=jnp.float32)
            images = images[:half_rows] + images[half_rows:]
            decay = jnp.sum(jnp.where(lane == head, decay_ref[...], 0.0), axis=1, keepdims=True)
            beta = jnp.sum(jnp.where(lane == head, beta_ref[...], 0.0), axis=1, keepdims=True)
            columns = pl.ds(pl.multiple_of(head * DK, DK), DK)
            v = v_ref[:, columns].astype(jnp.float32)
            kept = None
            weights, writes = [], []
            for t in range(DRAFTS):
                seen = rows(images, t) if kept is None else kept * rows(images, t)
                for s in range(t):
                    seen = seen + (weights[s] * along_key[s, t]) * writes[s]
                now = rows(decay, t)
                writes.append(rows(v, t) - now * seen)
                kept = now if kept is None else kept * now
                weights = [now * w for w in weights] + [rows(beta, t)]
                got = kept * rows(images, DRAFTS + t)
                for s in range(t + 1):
                    got = got + (weights[s] * along_query[s, t]) * writes[s]
                out_ref[t * beams : (t + 1) * beams, columns] = got.astype(jnp.bfloat16)
        return carry

    lax.fori_loop(first, last, one, 0)


def expert_kernel(
    n, x_ref, gate_hbm, up_hbm, down_hbm, qk_hbm, v_hbm, decay_ref, beta_ref, state_src,
    out_ref, delta_ref, rows_in, part, core_in, y_in, z_in,
    z_send, z_recv, y_send, y_recv, c_send, c_recv,
    core_send, core_recv, fold_send, fold_recv, last_send, last_recv, own_sem,
    gate_ref, up_ref, down_ref, qk_ref, v_ref, state_ref, state_send, state_recv,
):
    deep = n // 4
    width = out_ref.shape[1]
    count = out_ref.shape[0]
    me = lax.axis_index("ep")
    c = lax.rem(me, 2)
    y = lax.rem(me // 2, 2)
    z = me // 4

    def at(zz, yy, cc):
        return (zz * 2 + yy) * 2 + cc

    other = at(z, y, 1 - c)
    across = at(z, 1 - y, c)
    near = jnp.minimum(z, deep - 1 - z)
    turn = [z]
    for k in range(1, deep):
        close = z - (k + 1) // 2 if k % 2 else z + k // 2
        far = jnp.where(z > near, z - (k - near), z + (k - near))
        turn.append(jnp.where(k <= 2 * near, close, far))
    peers = [lax.rem(me + k, n) for k in range(1, n)]
    barrier = pltpu.get_barrier_semaphore()
    for peer in peers:
        pl.semaphore_signal(barrier, inc=1, device_id={"ep": peer}, device_id_type=MESH)
    pl.semaphore_wait(barrier, len(peers))

    def send(src, dst, s_sem, r_sem, peer):
        copy = pltpu.make_async_remote_copy(
            src_ref=src, dst_ref=dst, send_sem=s_sem, recv_sem=r_sem,
            device_id={"ep": peer}, device_id_type=MESH,
        )
        copy.start()
        return copy

    local = [
        pltpu.make_async_copy(src, dst, own_sem.at[i])
        for i, (src, dst) in enumerate((
            (x_ref, rows_in.at[me]), (gate_hbm, gate_ref), (up_hbm, up_ref),
            (down_hbm, down_ref), (qk_hbm, qk_ref), (v_hbm, v_ref),
            (state_src.at[me], state_ref.at[me]),
        ))
    ]
    y_copies = {0: send(x_ref, rows_in.at[me], y_send.at[0], y_recv.at[0], across)}

    def pass_on(src, block, origin, k, target):
        return pltpu.make_async_remote_copy(
            src_ref=src, dst_ref=rows_in.at[block], send_sem=z_send.at[k],
            recv_sem=z_recv.at[origin], device_id={"ep": at(target, y, c)}, device_id_type=MESH,
        )

    above, below = lax.rem(z + 1, deep), lax.rem(z + deep - 1, deep)

    @pl.when(z + 1 < deep)
    def _():
        pass_on(x_ref, me, z, 0, above).start()

    @pl.when(z > 0)
    def _():
        pass_on(x_ref, me, z, deep, below).start()

    c_copies = {(0, 0): send(x_ref, rows_in.at[me], c_send.at[0], c_recv.at[0], other)}
    for copy in local:
        copy.start()
    state_copies = {
        k: send(
            state_src.at[peers[k - 1]], state_ref.at[me], state_send.at[k], state_recv.at[k],
            peers[k - 1],
        )
        for k in range(1, n)
    }
    core_copies, fold_copies, last_copies = {}, {}, {}
    lanes = lax.broadcasted_iota(jnp.int32, (4 * count, MIX_COLUMNS), 1)
    picked = (lanes == me) | (lanes == me + n)

    def onward(k):
        block = at(turn[k], y, c)
        target = jnp.where(turn[k] < z, above, below)
        goes = jnp.where(turn[k] < z, z + 1 < deep, z > 0)
        return goes, pass_on(rows_in.at[block], block, turn[k], k, target)

    def stage(k):
        block = at(turn[k], y, c)
        goes, copy = onward(k)
        copy.wait_recv()

        @pl.when(goes)
        def _():
            copy.start()

        y_copies[k] = send(rows_in.at[block], rows_in.at[block], y_send.at[k], y_recv.at[k], across)
        c_copies[k, 0] = send(
            rows_in.at[block], rows_in.at[block], c_send.at[2 * k], c_recv.at[2 * k], other
        )

    key_heads = qk_ref.shape[1] // (2 * DK)

    def delta(first, last):
        delta_heads(
            qk_ref, v_ref, decay_ref, beta_ref, state_ref, delta_ref, first, last
        )

    def fold_y(k):
        y_here = at(turn[k], y, c)
        fold_copies[k].wait_recv()
        part[y_here] = (
            part[y_here].astype(jnp.float32) + y_in[k].astype(jnp.float32)
        ).astype(jnp.bfloat16)
        if k:
            last_copies[k] = send(
                part.at[y_here], z_in.at[z], last_send.at[k], last_recv.at[z], y_here
            )

    for k in range(deep):
        y_copies[k].wait_recv()
        block = at(turn[k], 1 - y, c)
        c_copies[k, 1] = send(
            rows_in.at[block], rows_in.at[block], c_send.at[2 * k + 1], c_recv.at[2 * k + 1], other
        )
        if k + 1 < deep:
            stage(k + 1)
        if k == 0:
            for copy in local:
                copy.wait()
        c_copies[k, 0].wait_recv()
        c_copies[k, 1].wait_recv()
        first = pl.multiple_of(turn[k] * 4, 4)
        rows = rows_in[pl.ds(first, 4)].reshape(4 * count, -1)
        mix = jnp.sum(
            jnp.where(picked, rows[:, width:].astype(jnp.float32), 0.0), axis=1, keepdims=True
        )
        rows = rows[:, :width]
        gate_val = jnp.dot(rows, gate_ref[...], preferred_element_type=jnp.float32)
        up_val = jnp.dot(rows, up_ref[...], preferred_element_type=jnp.float32)
        inner = (gate_val * jax.nn.sigmoid(gate_val) * up_val).astype(jnp.bfloat16)
        made = jnp.dot(inner, down_ref[...], preferred_element_type=jnp.float32)
        part[pl.ds(first, 4)] = (made * mix).astype(jnp.bfloat16).reshape(4, count, width)
        for yy in range(2):
            core_copies[k, yy] = send(
                part.at[at(turn[k], yy, 1 - c)], core_in.at[2 * k + yy],
                core_send.at[2 * k + yy], core_recv.at[2 * k + yy], other,
            )
        for yy in range(2):
            core_copies[k, yy].wait_recv()
            here = at(turn[k], yy, c)
            part[here] = (
                part[here].astype(jnp.float32) + core_in[2 * k + yy].astype(jnp.float32)
            ).astype(jnp.bfloat16)
        fold_copies[k] = send(
            part.at[at(turn[k], 1 - y, c)], y_in.at[k], fold_send.at[k], fold_recv.at[k], across
        )
        if k:
            fold_y(k - 1)
    for copy in state_copies.values():
        copy.wait_recv()
    delta(0, key_heads // 2)
    fold_y(deep - 1)
    delta(key_heads // 2, key_heads)
    total = part[me].astype(jnp.float32)
    for k in range(1, deep):
        pltpu.make_async_remote_copy(
            src_ref=part.at[me], dst_ref=z_in.at[turn[k]], send_sem=last_send.at[k],
            recv_sem=last_recv.at[turn[k]], device_id={"ep": other}, device_id_type=MESH,
        ).wait_recv()
        total = total + z_in[turn[k]].astype(jnp.float32)
    out_ref[...] = total.astype(jnp.bfloat16)
    @pl.when(z + 1 < deep)
    def _():
        pass_on(x_ref, me, z, 0, above).wait_send()

    @pl.when(z > 0)
    def _():
        pass_on(x_ref, me, z, deep, below).wait_send()

    for k in range(1, deep):
        goes, copy = onward(k)

        @pl.when(goes)
        def _():
            copy.wait_send()

    for group in (state_copies, y_copies, c_copies, core_copies, fold_copies, last_copies):
        for copy in group.values():
            copy.wait_send()


def routed_experts(packed, gate_w, up_w, down_w, qk, v, decay, beta, states, n):
    count = packed.shape[0]
    width = down_w.shape[1]
    deep = n // 4
    dma = pltpu.SemaphoreType.DMA
    return pl.pallas_call(
        functools.partial(expert_kernel, n),
        out_shape=(
            jax.ShapeDtypeStruct((count, width), jnp.bfloat16),
            jax.ShapeDtypeStruct(v.shape, jnp.bfloat16),
        ),
        in_specs=[
            pl.BlockSpec(memory_space=pl.ANY if i in (1, 2, 3, 4, 5, 8) else pltpu.VMEM)
            for i in range(9)
        ],
        out_specs=(pl.BlockSpec(memory_space=pltpu.VMEM), pl.BlockSpec(memory_space=pltpu.VMEM)),
        scratch_shapes=[
            pltpu.VMEM((n, count, packed.shape[1]), jnp.bfloat16),
            pltpu.VMEM((n, count, width), jnp.bfloat16),
            pltpu.VMEM((2 * deep, count, width), jnp.bfloat16),
            pltpu.VMEM((deep, count, width), jnp.bfloat16),
            pltpu.VMEM((deep, count, width), jnp.bfloat16),
            dma((deep + 1,)), dma((deep,)), dma((deep,)), dma((deep,)),
            dma((2 * deep,)), dma((2 * deep,)), dma((2 * deep,)), dma((2 * deep,)),
            dma((deep,)), dma((deep,)), dma((deep,)), dma((deep,)), dma((7,)),
            *(pltpu.VMEM(x.shape, jnp.bfloat16) for x in (gate_w, up_w, down_w, qk, v, states)),
            dma((n,)), dma((n,)),
        ],
        compiler_params=pltpu.CompilerParams(
            collective_id=1, has_side_effects=True, vmem_limit_bytes=50 * 1024 * 1024
        ),
    )(packed, gate_w, up_w, down_w, qk, v, decay, beta, states)


def on_device(
    page_key_value_codes,
    page_key_scales,
    page_value_scales,
    block_table,
    prompt_lengths,
    decode_owner,
    prefill_states,
    att_query,
    att_gate,
    draft_keys_values,
    out_weight,
    residual,
    norm_gain,
    router_weight,
    expert_routes,
    gate_weight,
    up_weight,
    down_weight,
    gdn_qk,
    gdn_v,
    gdn_decay,
    gdn_beta,
):
    devices = lax.axis_size("ep")
    device_id = lax.axis_index("ep")
    labels = jnp.arange(devices, dtype=jnp.int32)
    matches = (decode_owner[:, None] == labels[None, :]).astype(jnp.int32)
    inverse = jnp.sum(labels[:, None] * matches, axis=0)
    page_ids = block_table[inverse]
    scales = jnp.concatenate([page_key_scales, page_value_scales], axis=1)[page_ids]
    scales = jnp.repeat(scales, PAGE_POSITIONS, axis=1).transpose(0, 2, 1)
    scales = jnp.pad(scales, ((0, 0), (0, 16 - scales.shape[1]), (0, 0)))
    blank = jnp.zeros_like(scales)
    scales = jnp.where(
        device_id % 2 == 0,
        jnp.concatenate([scales, blank], axis=2),
        jnp.concatenate([blank, scales], axis=2),
    )
    codes = page_key_value_codes[page_ids]
    codes = codes.reshape(devices, -1, codes.shape[-1])
    states = prefill_states[inverse]
    length = prompt_lengths[inverse[device_id]]
    live = (jnp.arange(devices * codes.shape[1], dtype=jnp.int32) < length).astype(jnp.float32)[None]
    beam_total, draft_tokens, width = att_query.shape
    row_count = beam_total * draft_tokens

    def flat(x):
        return x.reshape(row_count, -1)

    def by_draft(x):
        return x.transpose(1, 0, 2).reshape(row_count, -1)

    experts = router_weight.shape[1]
    spare = MIX_COLUMNS - 2 * experts
    router = jnp.concatenate([router_weight, router_weight], axis=1)
    router = jnp.pad(router, ((0, 0), (0, spare)))
    named = jnp.any(
        flat(expert_routes)[:, :, None] == jnp.arange(experts, dtype=jnp.int32)[None, None, :],
        axis=1,
    ).astype(jnp.float32)
    named = jnp.pad(jnp.concatenate([named, named], axis=1), ((0, 0), (0, spare)))
    attn_mix, packed = attend(
        experts,
        flat(att_query),
        flat(att_gate),
        flat(draft_keys_values),
        codes,
        scales,
        live,
        out_weight,
        flat(residual),
        norm_gain.astype(jnp.float32)[None],
        router,
        named,
    )
    moe_out, gdn_out = routed_experts(
        packed, gate_weight[0], up_weight[0], down_weight[0],
        by_draft(gdn_qk), by_draft(gdn_v), by_draft(gdn_decay), by_draft(gdn_beta), states, devices,
    )
    return (
        attn_mix.reshape(att_query.shape),
        moe_out.reshape(att_query.shape),
        gdn_out.reshape(draft_tokens, beam_total, -1).transpose(1, 0, 2),
    )


def solution(mesh):
    placed = (
        P(("grp", "ep"), None, None),
        P(("grp", "ep"), None),
        P(("grp", "ep"), None),
        P("grp", "ep"),
        P("grp"),
        P("grp"),
        P("grp", "ep", None, None),
        P(("grp", "ep"), None, None),
        P(("grp", "ep"), None, None),
        P(("grp", "ep"), None, None),
        P(),
        P(("grp", "ep"), None, None),
        P(),
        P(),
        P(("grp", "ep"), None, None),
        P("ep", None, None),
        P("ep", None, None),
        P("ep", None, None),
        P(("grp", "ep"), None, None),
        P(("grp", "ep"), None, None),
        P(("grp", "ep"), None, None),
        P(("grp", "ep"), None, None),
    )
    return jax.shard_map(
        on_device,
        mesh=mesh,
        in_specs=placed,
        out_specs=(
            P(("grp", "ep"), None, None),
            P(("grp", "ep"), None, None),
            P(("grp", "ep"), None, None),
        ),
        check_vma=False,
    )
```
